256 devices in a mesh: blk: 8 (over z), col: 8 (over x, y_lo), rep: 4 (over y_hi, core).
Axes of the slice: x: 4, y: 4 (y_hi: 2, y_lo: 2; y = y_hi * 2 + y_lo), z: 8, core: 2. Of those that a mesh axis runs over, the one named last changes fastest.
Arguments:
- tokens: bfloat16 [4096, 18432], P(('blk', 'rep'), 'col'), may hold values from -6 to 6
- grad_out: bfloat16 [4096, 18432], P(('blk', 'rep'), 'col'), may hold values from -6 to 6
- w_in: bfloat16 [18432, 4608], P('col', 'blk'), may hold values from -0.046875 to 0.046875
- w_out: bfloat16 [4608, 18432], P('blk', 'col'), may hold values from -0.046875 to 0.046875
Outputs:
- grad_tokens: bfloat16 [4096, 18432], P(('blk', 'rep'), 'col')
- grad_in: bfloat16 [18432, 4608], P('col', 'blk')
- grad_outw: bfloat16 [4608, 18432], P('blk', 'col')
The draws below stay inside these ranges and needn't reach their ends.
All inputs are finite; a program needn't handle non-finite values.
Results may differ from the reference program's by a relative error of at most 0.029.
Values may be sent and summed in bfloat16 or wider, within the bound.
A program may use at most 128 MiB of HBM per device.

```python
import math
import jax
import jax.numpy as jnp

D = 18432
TOK_DEV = 128
FF = 4608
TOKENS = 4096
N_BLK = 8
N_REP = 4


def level_of(key, shape, shards, smallest, top_value):
    level = 1.0
    for position, parts in shards:
        draws = jax.random.uniform(jax.random.fold_in(jax.random.fold_in(key, 6), position), (parts,), jnp.float32, smallest / len(shards), top_value / len(shards))
        level = level * jnp.repeat(jnp.exp(draws), shape[position] // parts).reshape((-1,) + (1,) * (len(shape) - 1 - position))
    return level


def normal_values(stream_key, shape, deviation, bound, shards=(), kind=jnp.bfloat16):
    values = jax.random.normal(stream_key, shape, jnp.float32) * deviation
    if len(shards) > 0:
        values = level_of(stream_key, shape, shards, -0.22, 0.18) * values
    return jnp.clip(values, min=-bound, max=bound).astype(kind)


def setup_inputs(seed: int = 0) -> dict:
    key_of = jax.random.split(jax.random.key(seed), 5)
    tokens = normal_values(key_of[0], (TOKENS, D), 1.0, 6.0, ((0, 32), (1, 8)))
    grad_out = normal_values(key_of[1], (TOKENS, D), 1.0, 6.0, ((0, 32), (1, 8)))
    w_in = normal_values(key_of[2], (D, FF), D ** -0.5, 0.046875, ((0, 8), (1, 8)))
    w_out = normal_values(key_of[3], (FF, D), D ** -0.5, 0.046875, ((0, 8), (1, 8)))
    return {"tokens": tokens, "grad_out": grad_out, "w_in": w_in, "w_out": w_out}


def gelu_tanh(value):
    return jax.nn.gelu(value, approximate=True)

def reference(tokens, grad_out, w_in, w_out):
    preact = jnp.dot(tokens, w_in, preferred_element_type=jnp.float32)
    grad_hidden = jnp.einsum('td,fd->tf', grad_out.astype(jnp.float32), w_out.astype(jnp.float32))
    active, pull = jax.vjp(gelu_tanh, preact)
    hidden = active.astype(jnp.bfloat16)
    grad_pre = pull(grad_hidden)[0].astype(jnp.bfloat16)
    grad_tokens = jnp.einsum('tf,df->td', grad_pre.astype(jnp.float32), w_in.astype(jnp.float32)).astype(jnp.bfloat16)
    scale = 1.0 / math.sqrt(TOKENS)
    width = tokens.shape[1]
    hid = hidden.shape[1]
    tok_split = tokens.reshape(N_BLK, N_REP, TOK_DEV, width)
    out_split = grad_out.reshape(N_BLK, N_REP, TOK_DEV, width)
    hid_split = hidden.reshape(N_BLK, N_REP, TOK_DEV, hid)
    pre_split = grad_pre.reshape(N_BLK, N_REP, TOK_DEV, hid)
    total_in = jnp.zeros((width, hid), jnp.float32)
    total_out = jnp.zeros((hid, width), jnp.float32)
    for replica in range(N_REP):
        rows_tok = tok_split[:, replica].reshape(N_BLK * TOK_DEV, width)
        rows_out = out_split[:, replica].reshape(N_BLK * TOK_DEV, width)
        rows_hid = hid_split[:, replica].reshape(N_BLK * TOK_DEV, hid)
        rows_pre = pre_split[:, replica].reshape(N_BLK * TOK_DEV, hid)
        part_in = (jnp.dot(rows_tok.T, rows_pre, preferred_element_type=jnp.float32) * scale).astype(jnp.bfloat16)
        part_out = (jnp.dot(rows_hid.T, rows_out, preferred_element_type=jnp.float32) * scale).astype(jnp.bfloat16)
        total_in = total_in + part_in.astype(jnp.float32)
        total_out = total_out + part_out.astype(jnp.float32)
    return (grad_tokens, total_in.astype(jnp.bfloat16), total_out.astype(jnp.bfloat16))
```

```python
import functools
import math

import jax
import jax.numpy as jnp
from jax import lax
from jax.experimental import pallas as pl
from jax.experimental.pallas import tpu as pltpu
from jax.sharding import PartitionSpec as P

MESH = pl.DeviceIdType.MESH
F32, BF16 = jnp.float32, jnp.bfloat16
NB, NC = 8, 8
TD, HALF, SUB, RC = 128, 64, 32, 16
DL, FL = 2304, 576
DH = DL // 2
YJ = 3
CO, RI = DH // YJ, DH // YJ
HO, HI = FL // 2, RI // 2
GELU_C = math.sqrt(2.0 / math.pi)
GELU_A = 0.044715
Y_LEAD = 3


def dot_nn(a, b):
    return jnp.dot(a, b, preferred_element_type=F32)


def dot_nt(a, b):
    return lax.dot_general(a, b, (((1,), (1,)), ((), ())), preferred_element_type=F32)


def gelu(v):
    return 0.5 * v * (1.0 + jnp.tanh(GELU_C * (v + GELU_A * (v * v * v))))


def gelu_grad(v):
    th = jnp.tanh(GELU_C * (v + GELU_A * (v * v * v)))
    slope = GELU_C * (1.0 + (3.0 * GELU_A) * (v * v))
    return 0.5 * (1.0 + th) + 0.5 * v * (1.0 - th * th) * slope


def kernel(
    scale,
    tokens,
    grad_out,
    w_in,
    w_out,
    gt_out,
    gi_out,
    go_out,
    xs,
    wi,
    wo,
    tok_t,
    hid_t,
    act,
    part,
    share,
    pre,
    zst,
    zrb,
    gst,
    ss_o,
    sr_o,
    own_o,
    ys_o,
    yr_o,
    fin_o,
    ss_i,
    sr_i,
    own_i,
    ys_i,
    yr_i,
    fin_i,
    load_sem,
    zsend,
    zrecv,
    rs_send,
    rs_recv,
    ag_send,
    ag_recv,
    qsend,
    qrecv,
    ysem,
    out_sem,
    gt_sem,
):
    b, c, r = lax.axis_index("blk"), lax.axis_index("col"), lax.axis_index("rep")
    yh, core = r // 2, r % 2
    up, down = lax.rem(b + 1, NB), lax.rem(b + NB - 1, NB)
    ring = ((up, c, r), (down, c, r))
    sibling = (b, c, yh * 2 + (1 - core))
    partner = (b, c, (1 - yh) * 2 + core)

    def col_partner(k):
        return lax.rem(c + k, NC)

    loads = [
        pltpu.make_async_copy(tokens, xs.at[0, pl.ds(0, TD)], load_sem.at[0]),
        pltpu.make_async_copy(w_in, wi, load_sem.at[1]),
        pltpu.make_async_copy(grad_out, xs.at[1, pl.ds(0, TD)], load_sem.at[2]),
        pltpu.make_async_copy(w_out, wo, load_sem.at[3]),
    ]
    for copy in loads:
        copy.start()

    barrier = pltpu.get_barrier_semaphore()
    peers = list(ring) + [sibling, partner]
    peers += [(b, col_partner(k), r) for k in range(1, NC)]
    for peer in peers:
        pl.semaphore_signal(barrier, inc=1, device_id=peer, device_id_type=MESH)
    pl.semaphore_wait(barrier, len(peers))

    def hop(t, s, d, q):
        rows = d * HALF + q * SUB
        return pltpu.make_async_remote_copy(
            src_ref=xs.at[t, pl.ds(s * TD + rows, SUB)],
            dst_ref=xs.at[t, pl.ds((s + 1) * TD + rows, SUB)],
            send_sem=zsend.at[t, s, d, q],
            recv_sem=zrecv.at[t, s, d, q],
            device_id=ring[d],
            device_id_type=MESH,
        )

    def pass_on(t, s):
        for q in range(2):
            for d in range(2):
                hop(t, s - 1, d, q).wait_recv()

                @pl.when(s < NB - 1)
                def _():
                    hop(t, s, d, q).start()

    def rs_copy(t, s, k):
        p = col_partner(k)
        return pltpu.make_async_remote_copy(
            src_ref=part.at[t, s, pl.ds(p * RC, RC)],
            dst_ref=share.at[t, s, k - 1],
            send_sem=rs_send.at[t, s],
            recv_sem=rs_recv.at[t, s],
            device_id=(b, p, r),
            device_id_type=MESH,
        )

    def ag_copy(t, s, k):
        rows = pl.ds(s * TD + c * RC, RC)
        return pltpu.make_async_remote_copy(
            src_ref=act.at[t, rows],
            dst_ref=act.at[t, rows],
            send_sem=ag_send.at[t, s],
            recv_sem=ag_recv.at[t, s],
            device_id=(b, col_partner(k), r),
            device_id_type=MESH,
        )

    def wait_bytes(sem, ref):
        pltpu.make_async_copy(ref, ref, sem).wait()

    def multiply(t, s):
        x = xs[t, pl.ds(s * TD, TD)]
        p = dot_nn(x, wi[...]) if t == 0 else dot_nt(x, wo[...])
        part[t, s] = p.astype(BF16)
        for k in range(1, NC):
            rs_copy(t, s, k).start()

    def reduce(t, s):
        wait_bytes(rs_recv.at[t, s], share.at[t, s])
        total = part[t, s, pl.ds(c * RC, RC)].astype(F32)
        for k in range(NC - 1):
            total += share[t, s, k].astype(F32)
        if t == 0:
            pre[s] = total
            value = gelu(total)
        else:
            value = total * gelu_grad(pre[s])
        act[t, pl.ds(s * TD + c * RC, RC)] = value.astype(BF16)
        for k in range(1, NC):
            ag_copy(t, s, k).start()

    def arrived(t, s):
        wait_bytes(ag_recv.at[t, s], act.at[t, pl.ds(s * TD, (NC - 1) * RC)])
        if t == 0:
            cols = pl.ds(pl.multiple_of(s * TD, TD), TD)
            hid_t[:, cols] = act[t, pl.ds(s * TD, TD)].T

    def transpose_tokens(s):
        cols = pl.ds(pl.multiple_of(s * TD, TD), TD)
        tok_t[:, cols] = xs[0, pl.ds(s * TD, TD)].T

    loads[0].wait()
    for q in range(2):
        for d in range(2):
            hop(0, 0, d, q).start()
        if q == 0:
            for d in range(2):
                hop(0, 0, d, q).wait_send()
    loads[1].wait()
    loads[2].wait()

    def tokens_step(s, carry):
        @pl.when(s > 0)
        def _():
            pass_on(0, s)

        @pl.when(s == NB - 2)
        def _():
            for q in range(2):
                for d in range(2):
                    hop(1, 0, d, q).start()

        multiply(0, s)

        @pl.when(s > 0)
        def _():
            reduce(0, s - 1)

        @pl.when(s > 1)
        def _():
            arrived(0, s - 2)

        transpose_tokens(s)
        return carry

    lax.fori_loop(0, NB, tokens_step, 0)
    loads[3].wait()

    def grads_step(s, carry):
        @pl.when(s > 0)
        def _():
            pass_on(1, s)

        multiply(1, s)

        @pl.when(s == 0)
        def _():
            reduce(0, NB - 1)
            arrived(0, NB - 2)

        @pl.when(s == 1)
        def _():
            arrived(0, NB - 1)

        @pl.when(s > 0)
        def _():
            reduce(1, s - 1)

        @pl.when(s > 1)
        def _():
            arrived(1, s - 2)

        return carry

    lax.fori_loop(0, NB, grads_step, 0)

    kinds = (
        (ss_o, sr_o, own_o, ys_o, yr_o, fin_o, HO),
        (ss_i, sr_i, own_i, ys_i, yr_i, fin_i, HI),
    )

    def remote(src, dst, sems, device):
        return pltpu.make_async_remote_copy(
            src_ref=src,
            dst_ref=dst,
            send_sem=sems.at[0],
            recv_sem=sems.at[1],
            device_id=device,
            device_id_type=MESH,
        )

    def core_copy(n, j):
        return remote(kinds[n][0].at[j], kinds[n][1].at[j], ysem.at[n, j, 0], sibling)

    def y_copy(n, j):
        return remote(kinds[n][3].at[j], kinds[n][4].at[j], ysem.at[n, j, 1], partner)

    def fin_copy(n, j, which):
        fin, h = kinds[n][5], kinds[n][6]
        half = (1 - yh) if which == 2 else yh
        ref = fin.at[core, j, pl.ds(half * h, h)]
        return remote(ref, ref, ysem.at[n, j, 2 + which], partner if which == 0 else sibling)

    def block(n, j, k):
        if n == 0:
            cols = pl.ds(pl.multiple_of(k * DH + j * CO, 128), CO)
            return dot_nn(hid_t[...], xs[1, :, cols]) * scale
        return dot_nn(tok_t[pl.ds(k * DH + j * RI, RI)], act[1]) * scale

    def y_start(n, j):
        ss, _, own = kinds[n][:3]
        ss[j] = block(n, j, 1 - core).astype(BF16)
        core_copy(n, j).start()
        own[j] = block(n, j, core)

    def y_middle(n, j):
        _, sr, own, ys, _, _, h = kinds[n]
        core_copy(n, j).wait_recv()
        theirs, mine = pl.ds((1 - yh) * h, h), pl.ds(yh * h, h)
        ys[j] = (own[j, theirs] + sr[j, theirs].astype(F32)).astype(BF16)
        y_copy(n, j).start()
        own[j, mine] = own[j, mine] + sr[j, mine].astype(F32)

    def y_final(n, j):
        _, _, own, _, yr, fin, h = kinds[n]
        y_copy(n, j).wait_recv()
        mine = pl.ds(yh * h, h)
        fin[core, j, mine] = (own[j, mine] + yr[j].astype(F32)).astype(BF16)
        fin_copy(n, j, 0).start()
        fin_copy(n, j, 1).start()

    def out_copy(n, j, k):
        if n == 0:
            cols = pl.ds(pl.multiple_of(k * DH + j * CO, 128), CO)
            return pltpu.make_async_copy(fin_o.at[k, j], go_out.at[:, cols], out_sem.at[n, j, k])
        return pltpu.make_async_copy(fin_i.at[k, j], gi_out.at[pl.ds(k * DH + j * RI, RI)], out_sem.at[n, j, k])

    def y_forward(n, j):
        fin_copy(n, j, 0).wait_recv()
        fin_copy(n, j, 2).start()
        out_copy(n, j, core).start()

    def y_end(n, j):
        fin_copy(n, j, 1).wait_recv()
        fin_copy(n, j, 2).wait_recv()
        out_copy(n, j, 1 - core).start()

    def at_tile(step, j):
        for n in range(2):

            @pl.when((j >= n * YJ) & (j < (n + 1) * YJ))
            def _():
                step(n, j - n * YJ)

    def z_copy(k, h, d):
        rows = pl.ds(d * HALF, HALF)
        return pltpu.make_async_remote_copy(
            src_ref=zst.at[k, h, rows],
            dst_ref=zrb.at[k, h, rows],
            send_sem=qsend.at[k, h, d],
            recv_sem=qrecv.at[k, h, d],
            device_id=ring[1 - d],
            device_id_type=MESH,
        )

    def gt_copy(h):
        return pltpu.make_async_copy(gst.at[h], gt_out.at[:, pl.ds(h * DH, DH)], gt_sem.at[h])

    def z_slot(i):
        k, h = i // 2, i % 2
        s = NB - 1 - k
        value = dot_nt(act[1, pl.ds(s * TD, TD)], wi[pl.ds(h * DH, DH)])

        @pl.when(k == 0)
        def _():
            zst[k, h] = value.astype(BF16)

        @pl.when((k > 0) & (k < NB - 1))
        def _():
            for d in range(2):
                z_copy(k - 1, h, d).wait_recv()
            zst[k, h] = (value + zrb[k - 1, h].astype(F32)).astype(BF16)

        @pl.when(k < NB - 1)
        def _():
            for d in range(2):
                z_copy(k, h, d).start()

        @pl.when(k == NB - 1)
        def _():
            for d in range(2):
                z_copy(k - 1, h, d).wait_recv()
            gst[h] = (value + zrb[k - 1, h].astype(F32)).astype(BF16)

    def slot(g, carry):
        @pl.when(g == 1)
        def _():
            reduce(1, NB - 1)

        @pl.when(g == 2)
        def _():
            arrived(1, NB - 2)
            arrived(1, NB - 1)

        i = g - Y_LEAD

        @pl.when((i >= 0) & (i < 2 * NB))
        def _():
            z_slot(i)

        j = g // 3

        @pl.when(g % 3 == 0)
        def _():
            at_tile(y_start, j)

        @pl.when(g % 3 == 1)
        def _():
            at_tile(y_middle, j)

        @pl.when(g % 3 == 2)
        def _():
            at_tile(y_final, j - 1)
            at_tile(y_forward, j - 2)
            at_tile(y_end, j - 3)

        return carry

    lax.fori_loop(0, 3 * (2 * YJ + 3), slot, 0)
    for h in range(2):
        gt_copy(h).start()

    for h in range(2):
        gt_copy(h).wait()

    def drain_tiles(j, carry):
        for n in range(2):
            core_copy(n, j).wait_send()
            y_copy(n, j).wait_send()
            for which in range(3):
                fin_copy(n, j, which).wait_send()
            for k in range(2):
                out_copy(n, j, k).wait()
        return carry

    lax.fori_loop(0, YJ, drain_tiles, 0)

    def drain_hops(s, carry):
        for d in range(2):
            for q in range(2):
                for t in range(2):
                    if t == 0 and q == 0:

                        @pl.when(s > 0)
                        def _():
                            hop(t, s, d, q).wait_send()
                    else:
                        hop(t, s, d, q).wait_send()
                z_copy(s, q, d).wait_send()
        return carry

    lax.fori_loop(0, NB - 1, drain_hops, 0)

    def drain_sums(s, carry):
        for t in range(2):
            wait_bytes(rs_send.at[t, s], share.at[t, s])
            wait_bytes(ag_send.at[t, s], share.at[t, s])
        return carry

    lax.fori_loop(0, NB, drain_sums, 0)


def shards(tokens, grad_out, w_in, w_out):
    total_tokens = tokens.shape[0] * lax.axis_size("blk") * lax.axis_size("rep")
    scale = 1.0 / math.sqrt(total_tokens)
    any_space = pl.BlockSpec(memory_space=pl.ANY)
    dma = pltpu.SemaphoreType.DMA
    rows = NB * TD
    flops = 10 * rows * DL * FL
    return pl.pallas_call(
        functools.partial(kernel, scale),
        out_shape=(
            jax.ShapeDtypeStruct((TD, DL), BF16),
            jax.ShapeDtypeStruct((DL, FL), BF16),
            jax.ShapeDtypeStruct((FL, DL), BF16),
        ),
        in_specs=[any_space] * 4,
        out_specs=(any_space,) * 3,
        scratch_shapes=[
            pltpu.VMEM((2, rows, DL), BF16),
            pltpu.VMEM((DL, FL), BF16),
            pltpu.VMEM((FL, DL), BF16),
            pltpu.VMEM((DL, rows), BF16),
            pltpu.VMEM((FL, rows), BF16),
            pltpu.VMEM((2, rows, FL), BF16),
            pltpu.VMEM((2, NB, TD, FL), BF16),
            pltpu.VMEM((2, NB, NC - 1, RC, FL), BF16),
            pltpu.VMEM((NB, RC, FL), F32),
            pltpu.VMEM((NB - 1, 2, TD, DH), BF16),
            pltpu.VMEM((NB - 1, 2, TD, DH), BF16),
            pltpu.VMEM((2, TD, DH), BF16),
            pltpu.VMEM((YJ, FL, CO), BF16),
            pltpu.VMEM((YJ, FL, CO), BF16),
            pltpu.VMEM((YJ, FL, CO), F32),
            pltpu.VMEM((YJ, HO, CO), BF16),
            pltpu.VMEM((YJ, HO, CO), BF16),
            pltpu.VMEM((2, YJ, FL, CO), BF16),
            pltpu.VMEM((YJ, RI, FL), BF16),
            pltpu.VMEM((YJ, RI, FL), BF16),
            pltpu.VMEM((YJ, RI, FL), F32),
            pltpu.VMEM((YJ, HI, FL), BF16),
            pltpu.VMEM((YJ, HI, FL), BF16),
            pltpu.VMEM((2, YJ, RI, FL), BF16),
            dma((4,)),
            dma((2, NB - 1, 2, 2)),
            dma((2, NB - 1, 2, 2)),
            dma((2, NB)),
            dma((2, NB)),
            dma((2, NB)),
            dma((2, NB)),
            dma((NB - 1, 2, 2)),
            dma((NB - 1, 2, 2)),
            dma((2, YJ, 5, 2)),
            dma((2, YJ, 2)),
            dma((2,)),
        ],
        compiler_params=pltpu.CompilerParams(
            collective_id=0, has_side_effects=True, vmem_limit_bytes=62 * 2**20
        ),
        cost_estimate=pl.CostEstimate(
            flops=flops, bytes_accessed=16 * 2**20, transcendentals=4 * rows * FL // NC
        ),
    )(tokens, grad_out, w_in, w_out)


def solution(mesh):
    placed = (P(("blk", "rep"), "col"), P(("blk", "rep"), "col"), P("col", "blk"), P("blk", "col"))
    return jax.shard_map(
        shards,
        mesh=mesh,
        in_specs=placed,
        out_specs=(P(("blk", "rep"), "col"), P("col", "blk"), P("blk", "col")),
        check_vma=False,
    )
```

```python
import functools
import math

import jax
import jax.numpy as jnp
from jax import lax
from jax.experimental import pallas as pl
from jax.experimental.pallas import tpu as pltpu
from jax.sharding import PartitionSpec as P

MESH = pl.DeviceIdType.MESH
F32, BF16 = jnp.float32, jnp.bfloat16
NB, NC = 8, 8
TD, HALF, SUB, RC = 128, 64, 32, 16
DL, FL = 2304, 576
DH = DL // 2
YJ = 3
TC = DH // YJ
GELU_C = math.sqrt(2.0 / math.pi)
GELU_A = 0.044715
Y_LEAD = 3


def dot_nn(a, b):
    return jnp.dot(a, b, preferred_element_type=F32)


def dot_nt(a, b):
    return lax.dot_general(a, b, (((1,), (1,)), ((), ())), preferred_element_type=F32)


def gelu(v):
    return 0.5 * v * (1.0 + jnp.tanh(GELU_C * (v + GELU_A * (v * v * v))))


def gelu_grad(v):
    th = jnp.tanh(GELU_C * (v + GELU_A * (v * v * v)))
    slope = GELU_C * (1.0 + (3.0 * GELU_A) * (v * v))
    return 0.5 * (1.0 + th) + 0.5 * v * (1.0 - th * th) * slope


def kernel(
    scale,
    tokens,
    grad_out,
    w_in_t,
    w_out,
    gt_out,
    gi_out,
    go_out,
    xs,
    w,
    act_t,
    act,
    part,
    share,
    pre,
    zst,
    zrb,
    ss,
    sr,
    own,
    ys,
    yr,
    load_sem,
    zsend,
    zrecv,
    rs_send,
    rs_recv,
    ag_send,
    ag_recv,
    qsend,
    qrecv,
    ysem,
):
    b, c, r = lax.axis_index("blk"), lax.axis_index("col"), lax.axis_index("rep")
    yh, core = r // 2, r % 2
    up, down = lax.rem(b + 1, NB), lax.rem(b + NB - 1, NB)
    ring = ((up, c, r), (down, c, r))
    sibling = (b, c, yh * 2 + (1 - core))
    partner = (b, c, (1 - yh) * 2 + core)

    def col_partner(k):
        return lax.rem(c + k, NC)

    loads = [
        pltpu.make_async_copy(tokens, xs.at[0, pl.ds(0, TD)], load_sem.at[0]),
        pltpu.make_async_copy(w_in_t, w.at[0], load_sem.at[1]),
        pltpu.make_async_copy(grad_out, xs.at[1, pl.ds(0, TD)], load_sem.at[2]),
        pltpu.make_async_copy(w_out, w.at[1], load_sem.at[3]),
    ]
    for copy in loads:
        copy.start()

    barrier = pltpu.get_barrier_semaphore()
    peers = list(ring) + [sibling, partner]
    peers += [(b, col_partner(k), r) for k in range(1, NC)]
    for peer in peers:
        pl.semaphore_signal(barrier, inc=1, device_id=peer, device_id_type=MESH)
    pl.semaphore_wait(barrier, len(peers))

    def hop(t, s, d, q):
        rows = d * HALF + q * SUB
        return pltpu.make_async_remote_copy(
            src_ref=xs.at[t, pl.ds(s * TD + rows, SUB)],
            dst_ref=xs.at[t, pl.ds((s + 1) * TD + rows, SUB)],
            send_sem=zsend.at[t, s, d, q],
            recv_sem=zrecv.at[t, s, d, q],
            device_id=ring[d],
            device_id_type=MESH,
        )

    def pass_on(t, s):
        for q in range(2):
            for d in range(2):
                hop(t, s - 1, d, q).wait_recv()

                @pl.when(s < NB - 1)
                def _():
                    hop(t, s, d, q).start()

    def rs_copy(t, s, k):
        p = col_partner(k)
        return pltpu.make_async_remote_copy(
            src_ref=part.at[t, s, pl.ds(p * RC, RC)],
            dst_ref=share.at[t, s, k - 1],
            send_sem=rs_send.at[t, s],
            recv_sem=rs_recv.at[t, s],
            device_id=(b, p, r),
            device_id_type=MESH,
        )

    def ag_copy(t, s, k):
        rows = pl.ds(s * TD + c * RC, RC)
        return pltpu.make_async_remote_copy(
            src_ref=act.at[t, rows],
            dst_ref=act.at[t, rows],
            send_sem=ag_send.at[t, s],
            recv_sem=ag_recv.at[t, s],
            device_id=(b, col_partner(k), r),
            device_id_type=MESH,
        )

    def wait_bytes(sem, ref):
        pltpu.make_async_copy(ref, ref, sem).wait()

    def multiply(t, s):
        x = xs[t, pl.ds(s * TD, TD)]
        part[t, s] = dot_nt(x, w[t]).astype(BF16)
        for k in range(1, NC):
            rs_copy(t, s, k).start()

    def reduce(t, s):
        wait_bytes(rs_recv.at[t, s], share.at[t, s])
        total = part[t, s, pl.ds(c * RC, RC)].astype(F32)
        for k in range(NC - 1):
            total += share[t, s, k].astype(F32)
        if t == 0:
            pre[s] = total
            value = gelu(total)
        else:
            value = total * gelu_grad(pre[s])
        act[t, pl.ds(s * TD + c * RC, RC)] = value.astype(BF16)
        for k in range(1, NC):
            ag_copy(t, s, k).start()

    def arrived(t, s):
        wait_bytes(ag_recv.at[t, s], act.at[t, pl.ds(s * TD, (NC - 1) * RC)])
        cols = pl.ds(pl.multiple_of(s * TD, TD), TD)
        act_t[t, :, cols] = act[t, pl.ds(s * TD, TD)].T

    loads[0].wait()
    for q in range(2):
        for d in range(2):
            hop(0, 0, d, q).start()
        if q == 0:
            for d in range(2):
                hop(0, 0, d, q).wait_send()
    loads[1].wait()
    loads[2].wait()

    def tokens_step(s, carry):
        @pl.when(s > 0)
        def _():
            pass_on(0, s)

        @pl.when(s == NB - 2)
        def _():
            for q in range(2):
                for d in range(2):
                    hop(1, 0, d, q).start()

        multiply(0, s)

        @pl.when(s > 0)
        def _():
            reduce(0, s - 1)

        @pl.when(s > 1)
        def _():
            arrived(0, s - 2)

        return carry

    lax.fori_loop(0, NB, tokens_step, 0)
    loads[3].wait()

    def grads_step(s, carry):
        @pl.when(s > 0)
        def _():
            pass_on(1, s)

        multiply(1, s)

        @pl.when(s == 0)
        def _():
            reduce(0, NB - 1)
            arrived(0, NB - 2)

        @pl.when(s == 1)
        def _():
            arrived(0, NB - 1)

        @pl.when(s > 0)
        def _():
            reduce(1, s - 1)

        @pl.when(s > 1)
        def _():
            arrived(1, s - 2)

        return carry

    lax.fori_loop(0, NB, grads_step, 0)

    def remote(src, dst, sems, device):
        return pltpu.make_async_remote_copy(
            src_ref=src,
            dst_ref=dst,
            send_sem=sems.at[0],
            recv_sem=sems.at[1],
            device_id=device,
            device_id_type=MESH,
        )

    fin = (go_out, gi_out)

    def core_copy(n, j):
        return remote(ss.at[n, j], sr.at[n, j], ysem.at[n, j, 0], sibling)

    def y_copy(n, j):
        return remote(ys.at[n, j], yr.at[n, j], ysem.at[n, j, 1], partner)

    def tile_cols(j, k):
        return pl.ds(pl.multiple_of(k * DH + j * TC, 128), TC)

    def fin_copy(n, j):
        ref = fin[n].at[:, tile_cols(j, core)]
        return remote(ref, ref, ysem.at[n, j, 2], sibling)

    def block(n, j, k):
        return dot_nn(act_t[n], xs[1 - n, :, tile_cols(j, k)]) * scale

    def y_start(n, j):
        ss[n, j] = block(n, j, 1 - core).astype(BF16)
        core_copy(n, j).start()
        own[n, j] = block(n, j, core)

    def y_middle(n, j):
        core_copy(n, j).wait_recv()
        ys[n, j] = (own[n, j] + sr[n, j].astype(F32)).astype(BF16)
        y_copy(n, j).start()

    def y_final(n, j):
        y_copy(n, j).wait_recv()
        value = (ys[n, j].astype(F32) + yr[n, j].astype(F32)).astype(BF16)
        fin[n][:, tile_cols(j, core)] = value
        fin_copy(n, j).start()

    def y_end(n, j):
        fin_copy(n, j).wait_recv()

    def at_tile(step, j):
        for n in range(2):

            @pl.when((j >= n * YJ) & (j < (n + 1) * YJ))
            def _():
                step(n, j - n * YJ)

    def z_copy(k, h, d):
        rows = pl.ds(d * HALF, HALF)
        return pltpu.make_async_remote_copy(
            src_ref=zst.at[k, h, rows],
            dst_ref=zrb.at[k, h, rows],
            send_sem=qsend.at[k, h, d],
            recv_sem=qrecv.at[k, h, d],
            device_id=ring[1 - d],
            device_id_type=MESH,
        )

    def z_slot(i):
        k, h = i // 2, i % 2
        s = NB - 1 - k
        value = dot_nn(act[1, pl.ds(s * TD, TD)], w[0, :, pl.ds(pl.multiple_of(h * DH, 128), DH)])

        @pl.when(k == 0)
        def _():
            zst[k, h] = value.astype(BF16)

        @pl.when((k > 0) & (k < NB - 1))
        def _():
            for d in range(2):
                z_copy(k - 1, h, d).wait_recv()
            zst[k, h] = (value + zrb[k - 1, h].astype(F32)).astype(BF16)

        @pl.when(k < NB - 1)
        def _():
            for d in range(2):
                z_copy(k, h, d).start()

        @pl.when(k == NB - 1)
        def _():
            for d in range(2):
                z_copy(k - 1, h, d).wait_recv()
            gt_out[:, pl.ds(pl.multiple_of(h * DH, 128), DH)] = (value + zrb[k - 1, h].astype(F32)).astype(BF16)

    def slot(g, carry):
        @pl.when(g == 1)
        def _():
            reduce(1, NB - 1)

        @pl.when(g == 2)
        def _():
            arrived(1, NB - 2)
            arrived(1, NB - 1)

        i = g - Y_LEAD

        @pl.when((i >= 0) & (i < 2 * NB))
        def _():
            z_slot(i)

        j = g // 3

        @pl.when(g % 3 == 0)
        def _():
            at_tile(y_start, j)

        @pl.when(g % 3 == 1)
        def _():
            at_tile(y_middle, j)

        @pl.when(g % 3 == 2)
        def _():
            at_tile(y_final, j - 1)
            at_tile(y_end, j - 2)

        return carry

    lax.fori_loop(0, 3 * (2 * YJ + 2), slot, 0)


    def drain_tiles(j, carry):
        for n in range(2):
            core_copy(n, j).wait_send()
            y_copy(n, j).wait_send()
            fin_copy(n, j).wait_send()
        return carry

    lax.fori_loop(0, YJ, drain_tiles, 0)

    def drain_hops(s, carry):
        for d in range(2):
            for q in range(2):
                for t in range(2):
                    if t == 0 and q == 0:

                        @pl.when(s > 0)
                        def _():
                            hop(t, s, d, q).wait_send()
                    else:
                        hop(t, s, d, q).wait_send()
                z_copy(s, q, d).wait_send()
        return carry

    lax.fori_loop(0, NB - 1, drain_hops, 0)

    def drain_sums(s, carry):
        for t in range(2):
            wait_bytes(rs_send.at[t, s], share.at[t, s])
            wait_bytes(ag_send.at[t, s], share.at[t, s])
        return carry

    lax.fori_loop(0, NB, drain_sums, 0)


def shards(tokens, grad_out, w_in, w_out):
    total_tokens = tokens.shape[0] * lax.axis_size("blk") * lax.axis_size("rep")
    scale = 1.0 / math.sqrt(total_tokens)
    any_space = pl.BlockSpec(memory_space=pl.ANY)
    dma = pltpu.SemaphoreType.DMA
    rows = NB * TD
    flops = 10 * rows * DL * FL
    grad_tokens, grad_in_t, grad_outw = pl.pallas_call(
        functools.partial(kernel, scale),
        out_shape=(
            pltpu.VMEM((TD, DL), BF16),
            pltpu.VMEM((FL, DL), BF16),
            pltpu.VMEM((FL, DL), BF16),
        ),
        in_specs=[any_space] * 4,
        out_specs=(pl.BlockSpec(memory_space=pltpu.VMEM),) * 3,
        scratch_shapes=[
            pltpu.VMEM((2, rows, DL), BF16),
            pltpu.VMEM((2, FL, DL), BF16),
            pltpu.VMEM((2, FL, rows), BF16),
            pltpu.VMEM((2, rows, FL), BF16),
            pltpu.VMEM((2, NB, TD, FL), BF16),
            pltpu.VMEM((2, NB, NC - 1, RC, FL), BF16),
            pltpu.VMEM((NB, RC, FL), F32),
            pltpu.VMEM((NB - 1, 2, TD, DH), BF16),
            pltpu.VMEM((NB - 1, 2, TD, DH), BF16),
            pltpu.VMEM((2, YJ, FL, TC), BF16),
            pltpu.VMEM((2, YJ, FL, TC), BF16),
            pltpu.VMEM((2, YJ, FL, TC), F32),
            pltpu.VMEM((2, YJ, FL, TC), BF16),
            pltpu.VMEM((2, YJ, FL, TC), BF16),
            dma((4,)),
            dma((2, NB - 1, 2, 2)),
            dma((2, NB - 1, 2, 2)),
            dma((2, NB)),
            dma((2, NB)),
            dma((2, NB)),
            dma((2, NB)),
            dma((NB - 1, 2, 2)),
            dma((NB - 1, 2, 2)),
            dma((2, YJ, 3, 2)),
        ],
        compiler_params=pltpu.CompilerParams(
            collective_id=0, has_side_effects=True, vmem_limit_bytes=56 * 2**20
        ),
        cost_estimate=pl.CostEstimate(
            flops=flops, bytes_accessed=16 * 2**20, transcendentals=4 * rows * FL // NC
        ),
    )(tokens, grad_out, w_in.T, w_out)
    return grad_tokens, grad_in_t.T, grad_outw


def solution(mesh):
    placed = (P(("blk", "rep"), "col"), P(("blk", "rep"), "col"), P("col", "blk"), P("blk", "col"))
    return jax.shard_map(
        shards,
        mesh=mesh,
        in_specs=placed,
        out_specs=(P(("blk", "rep"), "col"), P("col", "blk"), P("blk", "col")),
        check_vma=False,
    )
```

```python
import functools
import math

import jax
import jax.numpy as jnp
from jax import lax
from jax.experimental import pallas as pl
from jax.experimental.pallas import tpu as pltpu
from jax.sharding import PartitionSpec as P

MESH = pl.DeviceIdType.MESH
F32, BF16 = jnp.float32, jnp.bfloat16
NB, NC = 8, 8
TD, HALF, SUB, RC = 128, 64, 32, 16
DL, FL = 2304, 576
DH = DL // 2
YJ = 3
TC = DH // YJ
CW = 2 * TC
PIECES = (
    (0, pl.ds(0, SUB), pl.ds(0, DL)),
    (0, pl.ds(SUB, SUB), pl.ds(0, DL)),
    (1, pl.ds(0, SUB), pl.ds(0, DL)),
    (1, pl.ds(SUB, SUB), pl.ds(0, DL)),
)
FIRST, SECOND = (0, 1), (2, 3)
GELU_C = math.sqrt(2.0 / math.pi)
GELU_A = 0.044715
LAG_SUM, LAG_ACT = 2, 4
LATE = 8
Y_LEAD = 2


def dot_nn(a, b):
    return jnp.dot(a, b, preferred_element_type=F32)


def dot_nt(a, b):
    return lax.dot_general(a, b, (((1,), (1,)), ((), ())), preferred_element_type=F32)


def gelu(v):
    return 0.5 * v * (1.0 + jnp.tanh(GELU_C * (v + GELU_A * (v * v * v))))


def gelu_grad(v):
    th = jnp.tanh(GELU_C * (v + GELU_A * (v * v * v)))
    slope = GELU_C * (1.0 + (3.0 * GELU_A) * (v * v))
    return 0.5 * (1.0 + th) + 0.5 * v * (1.0 - th * th) * slope


def kernel(
    scale,
    tokens,
    grad_out,
    w_in_t,
    w_out,
    gt_out,
    gi_out,
    go_out,
    xs,
    w,
    act_t,
    act,
    part,
    share,
    pre,
    zst,
    zrb,
    ss,
    sr,
    own,
    ys,
    yr,
    load_sem,
    zsend,
    zrecv,
    rs_send,
    rs_recv,
    ag_send,
    ag_recv,
    qsend,
    qrecv,
    ysem,
):
    b, c, r = lax.axis_index("blk"), lax.axis_index("col"), lax.axis_index("rep")
    yh, core = r // 2, r % 2
    up, down = lax.rem(b + 1, NB), lax.rem(b + NB - 1, NB)
    ring = ((up, c, r), (down, c, r))
    sibling = (b, c, yh * 2 + (1 - core))
    partner = (b, c, (1 - yh) * 2 + core)

    def col_partner(k):
        return lax.rem(c + k, NC)

    loads = [
        pltpu.make_async_copy(tokens, xs.at[0, pl.ds(0, TD)], load_sem.at[0]),
        pltpu.make_async_copy(w_in_t, w.at[0], load_sem.at[1]),
        pltpu.make_async_copy(grad_out, xs.at[1, pl.ds(0, TD)], load_sem.at[2]),
        pltpu.make_async_copy(w_out, w.at[1], load_sem.at[3]),
    ]
    for copy in loads:
        copy.start()

    barrier = pltpu.get_barrier_semaphore()
    peers = list(ring) + [sibling, partner]
    peers += [(b, col_partner(k), r) for k in range(1, NC)]
    for peer in peers:
        pl.semaphore_signal(barrier, inc=1, device_id=peer, device_id_type=MESH)
    pl.semaphore_wait(barrier, len(peers))

    def hop(q, s, d):
        t, rows, cols = PIECES[q]
        start = d * HALF + rows.start
        return pltpu.make_async_remote_copy(
            src_ref=xs.at[t, pl.ds(s * TD + start, rows.size), cols],
            dst_ref=xs.at[t, pl.ds((s + 1) * TD + start, rows.size), cols],
            send_sem=zsend.at[q, s, d],
            recv_sem=zrecv.at[q, s, d],
            device_id=ring[d],
            device_id_type=MESH,
        )

    def pass_on(pieces, s):
        for q in pieces:
            for d in range(2):
                hop(q, s - 1, d).wait_recv()

                @pl.when(s < NB - 1)
                def _():
                    hop(q, s, d).start()

    def rs_copy(t, s, k):
        p = col_partner(k)
        return pltpu.make_async_remote_copy(
            src_ref=part.at[t, s, pl.ds(p * RC, RC)],
            dst_ref=share.at[t, s, k - 1],
            send_sem=rs_send.at[t, s],
            recv_sem=rs_recv.at[t, s],
            device_id=(b, p, r),
            device_id_type=MESH,
        )

    def ag_copy(t, s, k):
        rows = pl.ds(s * TD + c * RC, RC)
        return pltpu.make_async_remote_copy(
            src_ref=act.at[t, rows],
            dst_ref=act.at[t, rows],
            send_sem=ag_send.at[t, s],
            recv_sem=ag_recv.at[t, s],
            device_id=(b, col_partner(k), r),
            device_id_type=MESH,
        )

    def wait_bytes(sem, ref):
        pltpu.make_async_copy(ref, ref, sem).wait()

    def multiply(t, s):
        x = xs[t, pl.ds(s * TD, TD)]
        part[t, s] = dot_nt(x, w[t]).astype(BF16)
        for k in range(1, NC):
            rs_copy(t, s, k).start()

    def reduce(t, s):
        wait_bytes(rs_recv.at[t, s], share.at[t, s])
        total = part[t, s, pl.ds(c * RC, RC)].astype(F32)
        for k in range(NC - 1):
            total += share[t, s, k].astype(F32)
        rows = pl.ds(s * TD + c * RC, RC)

        @pl.when(t == 0)
        def _():
            pre[s] = total
            act[0, rows] = gelu(total).astype(BF16)

        @pl.when(t == 1)
        def _():
            act[1, rows] = (total * gelu_grad(pre[s])).astype(BF16)

        for k in range(1, NC):
            ag_copy(t, s, k).start()

    def arrived(t, s):
        wait_bytes(ag_recv.at[t, s], act.at[t, pl.ds(s * TD, (NC - 1) * RC)])
        cols = pl.ds(pl.multiple_of(s * TD, TD), TD)
        act_t[t, :, cols] = act[t, pl.ds(s * TD, TD)].T

    def remote(src, dst, sems, device):
        return pltpu.make_async_remote_copy(
            src_ref=src,
            dst_ref=dst,
            send_sem=sems.at[0],
            recv_sem=sems.at[1],
            device_id=device,
            device_id_type=MESH,
        )

    fin = (go_out, gi_out)

    def core_copy(n, j):
        return remote(ss.at[n, j], sr.at[n, j], ysem.at[n, j, 0], sibling)

    def y_copy(n, j):
        return remote(ys.at[n, j], yr.at[n, j], ysem.at[n, j, 1], partner)

    def tile_cols(j, k):
        return pl.ds(pl.multiple_of(j * CW + k * TC, 128), TC)

    def fin_copy(n, j):
        ref = fin[n].at[:, tile_cols(j, core)]
        return remote(ref, ref, ysem.at[n, j, 2], sibling)

    def block(n, j, k):
        return dot_nn(act_t[n], xs[1 - n, :, tile_cols(j, k)]) * scale

    def y_give(n, j):
        ss[n, j] = block(n, j, 1 - core).astype(BF16)
        core_copy(n, j).start()

    def y_keep(n, j):
        own[n, j] = block(n, j, core)

    def y_start(n, j):
        y_give(n, j)
        y_keep(n, j)

    def y_middle(n, j):
        core_copy(n, j).wait_recv()
        ys[n, j] = (own[n, j] + sr[n, j].astype(F32)).astype(BF16)
        y_copy(n, j).start()

    def y_final(n, j):
        y_copy(n, j).wait_recv()
        value = (ys[n, j].astype(F32) + yr[n, j].astype(F32)).astype(BF16)
        fin[n][:, tile_cols(j, core)] = value
        fin_copy(n, j).start()

    def y_end(n, j):
        fin_copy(n, j).wait_recv()

    def at_tile(step, j):
        for n in range(2):

            @pl.when((j >= n * YJ) & (j < (n + 1) * YJ))
            def _():
                step(n, j - n * YJ)

    loads[0].wait()
    for d in range(2):
        hop(0, 0, d).start()
    for d in range(2):
        hop(0, 0, d).wait_send()
    for d in range(2):
        hop(1, 0, d).start()
    loads[2].wait()
    loads[1].wait()

    def gather_step(u, carry):
        t, s = u // NB, u % NB
        def pass_pieces(part_of):
            for n, pieces in enumerate((FIRST, SECOND)):

                @pl.when((t == n) & (s > 0))
                def _():
                    pass_on(part_of(pieces), s)

        pass_pieces(lambda pieces: pieces[:1])
        @pl.when(u == NB)
        def _():
            loads[3].wait()

        @pl.when(u >= LAG_SUM)
        def _():
            reduce((u - LAG_SUM) // NB, (u - LAG_SUM) % NB)

        @pl.when(u >= LAG_ACT)
        def _():
            arrived((u - LAG_ACT) // NB, (u - LAG_ACT) % NB)

        pass_pieces(lambda pieces: pieces[1:])

        @pl.when(u == NB - 2)
        def _():
            for q in SECOND:
                for d in range(2):
                    hop(q, 0, d).start()

        multiply(t, s)
        return carry

    lax.fori_loop(0, 2 * NB, gather_step, 0)

    def z_copy(k, h, d):
        rows = pl.ds(d * HALF, HALF)
        return pltpu.make_async_remote_copy(
            src_ref=zst.at[k, h, rows],
            dst_ref=zrb.at[k, h, rows],
            send_sem=qsend.at[k, h, d],
            recv_sem=qrecv.at[k, h, d],
            device_id=ring[1 - d],
            device_id_type=MESH,
        )

    def z_slot(i):
        k, h = i // 2, i % 2
        s = NB - 1 - k
        value = dot_nn(act[1, pl.ds(s * TD, TD)], w[0, :, pl.ds(pl.multiple_of(h * DH, 128), DH)])

        @pl.when(k == 0)
        def _():
            zst[k, h] = value.astype(BF16)

        @pl.when((k > 0) & (k < NB - 1))
        def _():
            for d in range(2):
                z_copy(k - 1, h, d).wait_recv()
            zst[k, h] = (value + zrb[k - 1, h].astype(F32)).astype(BF16)

        @pl.when(k < NB - 1)
        def _():
            for d in range(2):
                z_copy(k, h, d).start()

        @pl.when(k == NB - 1)
        def _():
            for d in range(2):
                z_copy(k - 1, h, d).wait_recv()
            gt_out[:, pl.ds(pl.multiple_of(h * DH, 128), DH)] = (value + zrb[k - 1, h].astype(F32)).astype(BF16)

    def slot(g, carry):
        @pl.when(g == 0)
        def _():
            reduce(1, NB - 2)
            arrived(1, NB - 4)

        @pl.when(g == 1)
        def _():
            reduce(1, NB - 1)
            arrived(1, NB - 3)

        @pl.when(g == 2)
        def _():
            arrived(1, NB - 2)
            arrived(1, NB - 1)

        i = g - Y_LEAD

        @pl.when((i >= 0) & (i < 2 * NB))
        def _():
            z_slot(i)

        j = g // 2

        @pl.when(g % 2 == 0)
        def _():
            at_tile(y_start, j)

        @pl.when(g % 2 == 1)
        def _():
            at_tile(y_middle, j)

        @pl.when((g % 2 == 0) & (g >= LATE))
        def _():
            at_tile(y_final, (g - LATE) // 2)
            at_tile(y_end, (g - LATE) // 2 - 1)

        return carry

    lax.fori_loop(0, LATE + 2 * (2 * YJ + 1), slot, 0)


    def drain_tiles(j, carry):
        for n in range(2):
            core_copy(n, j).wait_send()
            y_copy(n, j).wait_send()
            fin_copy(n, j).wait_send()
        return carry

    lax.fori_loop(0, YJ, drain_tiles, 0)

    def drain_hops(s, carry):
        for d in range(2):
            for q in range(len(PIECES)):
                if q == 0:

                    @pl.when(s > 0)
                    def _():
                        hop(q, s, d).wait_send()
                else:
                    hop(q, s, d).wait_send()
            for h in range(2):
                z_copy(s, h, d).wait_send()
        return carry

    lax.fori_loop(0, NB - 1, drain_hops, 0)

    def drain_sums(s, carry):
        for t in range(2):
            wait_bytes(rs_send.at[t, s], share.at[t, s])
            wait_bytes(ag_send.at[t, s], share.at[t, s])
        return carry

    lax.fori_loop(0, NB, drain_sums, 0)


def move_out(*refs):
    *pairs, sem = refs
    copies = []
    for n in range(3):
        src, dst = pairs[n], pairs[3 + n]
        rows = src.shape[0] // 2
        for h in range(2):
            part = pl.ds(h * rows, rows)
            copies.append(pltpu.make_async_copy(src.at[part], dst.at[part], sem.at[n, h]))
    for copy in copies:
        copy.start()
    for copy in copies:
        copy.wait()


def shards(tokens, grad_out, w_in, w_out):
    total_tokens = tokens.shape[0] * lax.axis_size("blk") * lax.axis_size("rep")
    scale = 1.0 / math.sqrt(total_tokens)
    any_space = pl.BlockSpec(memory_space=pl.ANY)
    dma = pltpu.SemaphoreType.DMA
    rows = NB * TD
    flops = 10 * rows * DL * FL
    grad_tokens, grad_in_t, grad_outw = pl.pallas_call(
        functools.partial(kernel, scale),
        out_shape=(
            pltpu.VMEM((TD, DL), BF16),
            pltpu.VMEM((FL, DL), BF16),
            pltpu.VMEM((FL, DL), BF16),
        ),
        in_specs=[any_space] * 4,
        out_specs=(pl.BlockSpec(memory_space=pltpu.VMEM),) * 3,
        scratch_shapes=[
            pltpu.VMEM((2, rows, DL), BF16),
            pltpu.VMEM((2, FL, DL), BF16),
            pltpu.VMEM((2, FL, rows), BF16),
            pltpu.VMEM((2, rows, FL), BF16),
            pltpu.VMEM((2, NB, TD, FL), BF16),
            pltpu.VMEM((2, NB, NC - 1, RC, FL), BF16),
            pltpu.VMEM((NB, RC, FL), F32),
            pltpu.VMEM((NB - 1, 2, TD, DH), BF16),
            pltpu.VMEM((NB - 1, 2, TD, DH), BF16),
            pltpu.VMEM((2, YJ, FL, TC), BF16),
            pltpu.VMEM((2, YJ, FL, TC), BF16),
            pltpu.VMEM((2, YJ, FL, TC), F32),
            pltpu.VMEM((2, YJ, FL, TC), BF16),
            pltpu.VMEM((2, YJ, FL, TC), BF16),
            dma((4,)),
            dma((len(PIECES), NB - 1, 2)),
            dma((len(PIECES), NB - 1, 2)),
            dma((2, NB)),
            dma((2, NB)),
            dma((2, NB)),
            dma((2, NB)),
            dma((NB - 1, 2, 2)),
            dma((NB - 1, 2, 2)),
            dma((2, YJ, 3, 2)),
        ],
        compiler_params=pltpu.CompilerParams(
            collective_id=0, has_side_effects=True, vmem_limit_bytes=56 * 2**20
        ),
        cost_estimate=pl.CostEstimate(
            flops=flops, bytes_accessed=16 * 2**20, transcendentals=4 * rows * FL // NC
        ),
    )(tokens, grad_out, w_in.T, w_out)
    grad_tokens, grad_in_t, grad_outw = pl.pallas_call(
        move_out,
        out_shape=(
            jax.ShapeDtypeStruct((TD, DL), BF16),
            jax.ShapeDtypeStruct((FL, DL), BF16),
            jax.ShapeDtypeStruct((FL, DL), BF16),
        ),
        in_specs=[pl.BlockSpec(memory_space=pltpu.VMEM)] * 3,
        out_specs=(any_space,) * 3,
        scratch_shapes=[dma((3, 2))],
        compiler_params=pltpu.CompilerParams(vmem_limit_bytes=8 * 2**20),
    )(grad_tokens, grad_in_t, grad_outw)
    return grad_tokens, grad_in_t.T, grad_outw


def solution(mesh):
    placed = (P(("blk", "rep"), "col"), P(("blk", "rep"), "col"), P("col", "blk"), P("blk", "col"))
    return jax.shard_map(
        shards,
        mesh=mesh,
        in_specs=placed,
        out_specs=(P(("blk", "rep"), "col"), P("col", "blk"), P("blk", "col")),
        check_vma=False,
    )
```

```python
import functools
import math

import jax
import jax.numpy as jnp
from jax import lax
from jax.experimental import pallas as pl
from jax.experimental.pallas import tpu as pltpu
from jax.sharding import PartitionSpec as P

MESH = pl.DeviceIdType.MESH
F32, BF16 = jnp.float32, jnp.bfloat16
NB, NC = 8, 8
TD, HALF, SUB, RC = 128, 64, 32, 16
DL, FL = 2304, 576
DH = DL // 2
YJ = 3
TC = DH // YJ
CW = 2 * TC
PIECES = (
    (0, pl.ds(0, SUB), pl.ds(0, DL)),
    (0, pl.ds(SUB, SUB), pl.ds(0, DL)),
    (1, pl.ds(0, SUB), pl.ds(0, DL)),
    (1, pl.ds(SUB, SUB), pl.ds(0, DL)),
)
FIRST, SECOND = (0, 1), (2, 3)
GELU_C = math.sqrt(2.0 / math.pi)
GELU_A = 0.044715
LAG_SUM, LAG_ACT = 2, 4
LATE = 8
Y_LEAD = 2


def dot_nn(a, b):
    return jnp.dot(a, b, preferred_element_type=F32)


def dot_nt(a, b):
    return lax.dot_general(a, b, (((1,), (1,)), ((), ())), preferred_element_type=F32)


def gelu(v):
    return 0.5 * v * (1.0 + jnp.tanh(GELU_C * (v + GELU_A * (v * v * v))))


def gelu_grad(v):
    th = jnp.tanh(GELU_C * (v + GELU_A * (v * v * v)))
    slope = GELU_C * (1.0 + (3.0 * GELU_A) * (v * v))
    return 0.5 * (1.0 + th) + 0.5 * v * (1.0 - th * th) * slope


def kernel(
    scale,
    tokens,
    grad_out,
    w_in_t,
    w_out,
    gt_out,
    gi_out,
    go_out,
    xs,
    w,
    act_t,
    act,
    part,
    share,
    pre,
    zst,
    zrb,
    ss,
    sr,
    own,
    ys,
    yr,
    load_sem,
    zsend,
    zrecv,
    rs_send,
    rs_recv,
    ag_send,
    ag_recv,
    qsend,
    qrecv,
    ysem,
):
    b, c, r = lax.axis_index("blk"), lax.axis_index("col"), lax.axis_index("rep")
    yh, core = r // 2, r % 2
    up, down = lax.rem(b + 1, NB), lax.rem(b + NB - 1, NB)
    ring = ((up, c, r), (down, c, r))
    sibling = (b, c, yh * 2 + (1 - core))
    partner = (b, c, (1 - yh) * 2 + core)

    def col_partner(k):
        return lax.rem(c + k, NC)

    loads = [
        pltpu.make_async_copy(tokens, xs.at[0, pl.ds(0, TD)], load_sem.at[0]),
        pltpu.make_async_copy(w_in_t, w.at[0], load_sem.at[1]),
        pltpu.make_async_copy(grad_out, xs.at[1, pl.ds(0, TD)], load_sem.at[2]),
        pltpu.make_async_copy(w_out, w.at[1], load_sem.at[3]),
    ]
    loads[0].start()

    barrier = pltpu.get_barrier_semaphore()
    peers = list(ring) + [sibling, partner]
    peers += [(b, col_partner(k), r) for k in range(1, NC)]
    for peer in peers:
        pl.semaphore_signal(barrier, inc=1, device_id=peer, device_id_type=MESH)
    pl.semaphore_wait(barrier, len(peers))

    def hop(q, s, d):
        t, rows, cols = PIECES[q]
        start = d * HALF + rows.start
        return pltpu.make_async_remote_copy(
            src_ref=xs.at[t, pl.ds(s * TD + start, rows.size), cols],
            dst_ref=xs.at[t, pl.ds((s + 1) * TD + start, rows.size), cols],
            send_sem=zsend.at[q, s, d],
            recv_sem=zrecv.at[q, s, d],
            device_id=ring[d],
            device_id_type=MESH,
        )

    def pass_on(pieces, s):
        for q in pieces:
            for d in range(2):
                hop(q, s - 1, d).wait_recv()

                @pl.when(s < NB - 1)
                def _():
                    hop(q, s, d).start()

    def rs_copy(t, s, k):
        p = col_partner(k)
        return pltpu.make_async_remote_copy(
            src_ref=part.at[t, s, pl.ds(p * RC, RC)],
            dst_ref=share.at[t, s, k - 1],
            send_sem=rs_send.at[t, s],
            recv_sem=rs_recv.at[t, s],
            device_id=(b, p, r),
            device_id_type=MESH,
        )

    def ag_copy(t, s, k):
        rows = pl.ds(s * TD + c * RC, RC)
        return pltpu.make_async_remote_copy(
            src_ref=act.at[t, rows],
            dst_ref=act.at[t, rows],
            send_sem=ag_send.at[t, s],
            recv_sem=ag_recv.at[t, s],
            device_id=(b, col_partner(k), r),
            device_id_type=MESH,
        )

    def wait_bytes(sem, ref):
        pltpu.make_async_copy(ref, ref, sem).wait()

    def multiply(t, s):
        x = xs[t, pl.ds(s * TD, TD)]
        part[t, s] = dot_nt(x, w[t]).astype(BF16)
        for k in range(1, NC):
            rs_copy(t, s, k).start()

    def reduce(t, s):
        wait_bytes(rs_recv.at[t, s], share.at[t, s])
        total = part[t, s, pl.ds(c * RC, RC)].astype(F32)
        for k in range(NC - 1):
            total += share[t, s, k].astype(F32)
        rows = pl.ds(s * TD + c * RC, RC)

        @pl.when(t == 0)
        def _():
            pre[s] = total
            act[0, rows] = gelu(total).astype(BF16)

        @pl.when(t == 1)
        def _():
            act[1, rows] = (total * gelu_grad(pre[s])).astype(BF16)

        for k in range(1, NC):
            ag_copy(t, s, k).start()

    def arrived(t, s):
        wait_bytes(ag_recv.at[t, s], act.at[t, pl.ds(s * TD, (NC - 1) * RC)])
        cols = pl.ds(pl.multiple_of(s * TD, TD), TD)
        act_t[t, :, cols] = act[t, pl.ds(s * TD, TD)].T

    def remote(src, dst, sems, device):
        return pltpu.make_async_remote_copy(
            src_ref=src,
            dst_ref=dst,
            send_sem=sems.at[0],
            recv_sem=sems.at[1],
            device_id=device,
            device_id_type=MESH,
        )

    fin = (go_out, gi_out)

    def core_copy(n, j):
        return remote(ss.at[n, j], sr.at[n, j], ysem.at[n, j, 0], sibling)

    def y_copy(n, j):
        return remote(ys.at[n, j], yr.at[n, j], ysem.at[n, j, 1], partner)

    def tile_cols(j, k):
        return pl.ds(pl.multiple_of(j * CW + k * TC, 128), TC)

    def fin_copy(n, j):
        ref = fin[n].at[:, tile_cols(j, core)]
        return remote(ref, ref, ysem.at[n, j, 2], sibling)

    def block(n, j, k):
        return dot_nn(act_t[n], xs[1 - n, :, tile_cols(j, k)]) * scale

    def y_give(n, j):
        ss[n, j] = block(n, j, 1 - core).astype(BF16)
        core_copy(n, j).start()

    def y_keep(n, j):
        own[n, j] = block(n, j, core)

    def y_start(n, j):
        y_give(n, j)
        y_keep(n, j)

    def y_middle(n, j):
        core_copy(n, j).wait_recv()
        ys[n, j] = (own[n, j] + sr[n, j].astype(F32)).astype(BF16)
        y_copy(n, j).start()

    def y_final(n, j):
        y_copy(n, j).wait_recv()
        value = (ys[n, j].astype(F32) + yr[n, j].astype(F32)).astype(BF16)
        fin[n][:, tile_cols(j, core)] = value
        fin_copy(n, j).start()

    def y_end(n, j):
        fin_copy(n, j).wait_recv()

    def at_tile(step, j):
        for n in range(2):

            @pl.when((j >= n * YJ) & (j < (n + 1) * YJ))
            def _():
                step(n, j - n * YJ)

    loads[0].wait()
    for d in range(2):
        hop(0, 0, d).start()
    for copy in loads[1:]:
        copy.start()
    for d in range(2):
        hop(0, 0, d).wait_send()
    for d in range(2):
        hop(1, 0, d).start()
    loads[2].wait()
    loads[1].wait()

    def gather_step(u, carry):
        t, s = u // NB, u % NB
        def pass_pieces(part_of):
            for n, pieces in enumerate((FIRST, SECOND)):

                @pl.when((t == n) & (s > 0))
                def _():
                    pass_on(part_of(pieces), s)

        pass_pieces(lambda pieces: pieces[:1])
        @pl.when(u == NB)
        def _():
            loads[3].wait()

        @pl.when(u >= LAG_SUM)
        def _():
            reduce((u - LAG_SUM) // NB, (u - LAG_SUM) % NB)

        @pl.when(u >= LAG_ACT)
        def _():
            arrived((u - LAG_ACT) // NB, (u - LAG_ACT) % NB)

        pass_pieces(lambda pieces: pieces[1:])

        @pl.when(u == NB - 2)
        def _():
            for q in SECOND:
                for d in range(2):
                    hop(q, 0, d).start()

        multiply(t, s)
        return carry

    lax.fori_loop(0, 2 * NB, gather_step, 0)

    def z_copy(k, h, d):
        rows = pl.ds(d * HALF, HALF)
        return pltpu.make_async_remote_copy(
            src_ref=zst.at[k, h, rows],
            dst_ref=zrb.at[k, h, rows],
            send_sem=qsend.at[k, h, d],
            recv_sem=qrecv.at[k, h, d],
            device_id=ring[1 - d],
            device_id_type=MESH,
        )

    def z_slot(i):
        k, h = i // 2, i % 2
        s = NB - 1 - k
        value = dot_nn(act[1, pl.ds(s * TD, TD)], w[0, :, pl.ds(pl.multiple_of(h * DH, 128), DH)])

        @pl.when(k == 0)
        def _():
            zst[k, h] = value.astype(BF16)

        @pl.when((k > 0) & (k < NB - 1))
        def _():
            for d in range(2):
                z_copy(k - 1, h, d).wait_recv()
            zst[k, h] = (value + zrb[k - 1, h].astype(F32)).astype(BF16)

        @pl.when(k < NB - 1)
        def _():
            for d in range(2):
                z_copy(k, h, d).start()

        @pl.when(k == NB - 1)
        def _():
            for d in range(2):
                z_copy(k - 1, h, d).wait_recv()
            gt_out[:, pl.ds(pl.multiple_of(h * DH, 128), DH)] = (value + zrb[k - 1, h].astype(F32)).astype(BF16)

    def slot(g, carry):
        @pl.when(g == 0)
        def _():
            reduce(1, NB - 2)
            arrived(1, NB - 4)

        @pl.when(g == 1)
        def _():
            reduce(1, NB - 1)
            arrived(1, NB - 3)

        @pl.when(g == 2)
        def _():
            arrived(1, NB - 2)
            arrived(1, NB - 1)

        i = g - Y_LEAD

        @pl.when((i >= 0) & (i < 2 * NB))
        def _():
            z_slot(i)

        j = g // 2

        @pl.when(g % 2 == 0)
        def _():
            at_tile(y_start, j)

        @pl.when(g % 2 == 1)
        def _():
            at_tile(y_middle, j)

        @pl.when((g % 2 == 0) & (g >= LATE))
        def _():
            at_tile(y_final, (g - LATE) // 2)
            at_tile(y_end, (g - LATE) // 2 - 1)

        return carry

    lax.fori_loop(0, LATE + 2 * (2 * YJ + 1), slot, 0)


    def drain_tiles(j, carry):
        for n in range(2):
            core_copy(n, j).wait_send()
            y_copy(n, j).wait_send()
            fin_copy(n, j).wait_send()
        return carry

    lax.fori_loop(0, YJ, drain_tiles, 0)

    def drain_hops(s, carry):
        for d in range(2):
            for q in range(len(PIECES)):
                if q == 0:

                    @pl.when(s > 0)
                    def _():
                        hop(q, s, d).wait_send()
                else:
                    hop(q, s, d).wait_send()
            for h in range(2):
                z_copy(s, h, d).wait_send()
        return carry

    lax.fori_loop(0, NB - 1, drain_hops, 0)

    def drain_sums(s, carry):
        for t in range(2):
            wait_bytes(rs_send.at[t, s], share.at[t, s])
            wait_bytes(ag_send.at[t, s], share.at[t, s])
        return carry

    lax.fori_loop(0, NB, drain_sums, 0)


def move_out(*refs):
    *pairs, sem = refs
    copies = []
    for n in range(3):
        src, dst = pairs[n], pairs[3 + n]
        rows = src.shape[0] // 2
        for h in range(2):
            part = pl.ds(h * rows, rows)
            copies.append(pltpu.make_async_copy(src.at[part], dst.at[part], sem.at[n, h]))
    for copy in copies:
        copy.start()
    for copy in copies:
        copy.wait()


def shards(tokens, grad_out, w_in, w_out):
    total_tokens = tokens.shape[0] * lax.axis_size("blk") * lax.axis_size("rep")
    scale = 1.0 / math.sqrt(total_tokens)
    any_space = pl.BlockSpec(memory_space=pl.ANY)
    dma = pltpu.SemaphoreType.DMA
    rows = NB * TD
    flops = 10 * rows * DL * FL
    grad_tokens, grad_in_t, grad_outw = pl.pallas_call(
        functools.partial(kernel, scale),
        out_shape=(
            pltpu.VMEM((TD, DL), BF16),
            pltpu.VMEM((FL, DL), BF16),
            pltpu.VMEM((FL, DL), BF16),
        ),
        in_specs=[any_space] * 4,
        out_specs=(pl.BlockSpec(memory_space=pltpu.VMEM),) * 3,
        scratch_shapes=[
            pltpu.VMEM((2, rows, DL), BF16),
            pltpu.VMEM((2, FL, DL), BF16),
            pltpu.VMEM((2, FL, rows), BF16),
            pltpu.VMEM((2, rows, FL), BF16),
            pltpu.VMEM((2, NB, TD, FL), BF16),
            pltpu.VMEM((2, NB, NC - 1, RC, FL), BF16),
            pltpu.VMEM((NB, RC, FL), F32),
            pltpu.VMEM((NB - 1, 2, TD, DH), BF16),
            pltpu.VMEM((NB - 1, 2, TD, DH), BF16),
            pltpu.VMEM((2, YJ, FL, TC), BF16),
            pltpu.VMEM((2, YJ, FL, TC), BF16),
            pltpu.VMEM((2, YJ, FL, TC), F32),
            pltpu.VMEM((2, YJ, FL, TC), BF16),
            pltpu.VMEM((2, YJ, FL, TC), BF16),
            dma((4,)),
            dma((len(PIECES), NB - 1, 2)),
            dma((len(PIECES), NB - 1, 2)),
            dma((2, NB)),
            dma((2, NB)),
            dma((2, NB)),
            dma((2, NB)),
            dma((NB - 1, 2, 2)),
            dma((NB - 1, 2, 2)),
            dma((2, YJ, 3, 2)),
        ],
        compiler_params=pltpu.CompilerParams(
            collective_id=0, has_side_effects=True, vmem_limit_bytes=56 * 2**20
        ),
        cost_estimate=pl.CostEstimate(
            flops=flops, bytes_accessed=16 * 2**20, transcendentals=4 * rows * FL // NC
        ),
    )(tokens, grad_out, w_in.T, w_out)
    grad_tokens, grad_in_t, grad_outw = pl.pallas_call(
        move_out,
        out_shape=(
            jax.ShapeDtypeStruct((TD, DL), BF16),
            jax.ShapeDtypeStruct((FL, DL), BF16),
            jax.ShapeDtypeStruct((FL, DL), BF16),
        ),
        in_specs=[pl.BlockSpec(memory_space=pltpu.VMEM)] * 3,
        out_specs=(any_space,) * 3,
        scratch_shapes=[dma((3, 2))],
        compiler_params=pltpu.CompilerParams(vmem_limit_bytes=8 * 2**20),
    )(grad_tokens, grad_in_t, grad_outw)
    return grad_tokens, grad_in_t.T, grad_outw


def solution(mesh):
    placed = (P(("blk", "rep"), "col"), P(("blk", "rep"), "col"), P("col", "blk"), P("blk", "col"))
    return jax.shard_map(
        shards,
        mesh=mesh,
        in_specs=placed,
        out_specs=(P(("blk", "rep"), "col"), P("col", "blk"), P("blk", "col")),
        check_vma=False,
    )
```
